128 devices in a mesh: dp: 8 (over y, core), block: 16 (over z, x).
Axes of the slice: x: 4, y: 4, z: 4, core: 2. Of those that a mesh axis runs over, the one named last changes fastest.
Arguments:
- activations: bfloat16 [128, 512, 2048], P(('dp', 'block')), may hold values from -6 to 6
- gradients: bfloat16 [128, 512, 2048], P(('dp', 'block')), may hold values from -6 to 6
- counts: int32 [128], P(('dp', 'block')), may hold values from 1 to 512, 32768 in all
- in_basis: bfloat16 [2048, 2048], replicated, may hold values from -0.125 to 0.125
- out_basis: bfloat16 [2048, 2048], replicated, may hold values from -0.125 to 0.125
- previous: float32 [4, 512, 2048], P(None, 'dp'), may hold values from 0.1 to 1
Outputs:
- corrections: float32 [4, 512, 2048], P(None, 'dp')
The draws below stay inside these ranges and needn't reach their ends.
Inputs may be any that keep to these rules, and one draw needn't show every extreme that they name: `counts`: some sequence has exactly 512 tokens.
All inputs are finite; a program needn't handle non-finite values. No bound on the sum of `counts` on one device may be relied on, other than what follows from the above.
Results may differ from the reference program's by a relative error of at most 0.00089.
Values may be sent and summed in bfloat16 or wider, within the bound.
A program may use at most 192 MiB of HBM per device.

```python
import math
import jax
import jax.numpy as jnp
import numpy as np
from jax import lax

ORDER = 2048
SEQ_LEN = 512
GRID_ROWS = 4
TILE_R = 512
SEQS = 128


def level_of(own_key, dims, split, low, high):
    def one(position, shards_of):
        heights = jax.random.uniform(jax.random.fold_in(jax.random.fold_in(own_key, 6), position), (shards_of,), jnp.float32, low / len(split), high / len(split))
        return jnp.repeat(jnp.exp(heights), dims[position] // shards_of).reshape((-1,) + (1,) * (len(dims) - position - 1))

    factor_of = one(*split[0])
    for cut in split[1:]:
        factor_of = factor_of * one(*cut)
    return factor_of


def split_up(number_of, total, bound, skew):
    portions = [(1 << 20) // math.isqrt(standing ** skew) + 1 for standing in range(2, number_of + 1)]
    rest, holding = total - bound - (number_of - 1), [1] * (number_of - 1)
    while rest > 0:
        candidates = [i for i in range(number_of - 1) if holding[i] < bound]
        pool, left = sum([portions[i] for i in candidates]), rest
        for i in candidates:
            more = min(bound - holding[i], max(1, left * portions[i] // pool), rest)
            holding[i] = holding[i] + more
            rest = rest - more
    return np.array([bound] + holding)


def uneven(rng, count, total, bound, skew):
    if count == 2:
        one = jax.random.randint(rng, (), max(1, total - bound), min(bound, total - 1) + 1)
        return jnp.stack([one, total - one])
    tallies = jnp.asarray(split_up(count, total, bound, skew), jnp.int32)
    couples = (count - 1) // 2
    source_of, receiver = tallies[1:1 + 2 * couples:2], tallies[2:2 + 2 * couples:2]
    slack = jnp.minimum(source_of - 1, bound - receiver)
    moved = jax.random.randint(jax.random.fold_in(rng, 1), (couples,), 0, 1 << 20) % (slack + 1)
    tallies = tallies.at[1:1 + 2 * couples:2].set(source_of - moved).at[2:2 + 2 * couples:2].set(receiver + moved)
    return tallies[jax.random.permutation(jax.random.fold_in(rng, 2), count)]


def bell_draw(key, extent, deviation, limit, split=(), held_as=jnp.bfloat16):
    values = deviation * jax.random.normal(key, extent, jnp.float32)
    if split:
        values = values * level_of(key, extent, split, -0.22, 0.18)
    return jnp.clip(values, -limit, limit).astype(held_as)


def setup_inputs(seed: int = 0) -> dict:
    splits = jax.random.split(jax.random.key(seed), 7)
    activations = bell_draw(splits[0], (SEQS, SEQ_LEN, ORDER), 1.0, 6.0, ((0, 128),))
    gradients = bell_draw(splits[1], (SEQS, SEQ_LEN, ORDER), 1.0, 6.0, ((0, 128),))
    counts = uneven(splits[2], SEQS, SEQS * SEQ_LEN // 2, SEQ_LEN, 2).astype(jnp.int32)
    in_basis = bell_draw(splits[3], (ORDER, ORDER), ORDER ** -0.5, 0.125)
    out_basis = bell_draw(splits[4], (ORDER, ORDER), ORDER ** -0.5, 0.125)
    previous = jnp.clip(jnp.exp(math.log(1.0) - 2.3025851 * jax.random.uniform(splits[5], (GRID_ROWS, TILE_R, ORDER), jnp.float32) ** level_of(splits[5], (GRID_ROWS, TILE_R, ORDER), ((1, 8),), -0.2, 0.2)), 0.1, 1.0)
    return dict(activations=activations, gradients=gradients, counts=counts, in_basis=in_basis, out_basis=out_basis, previous=previous)


def reference(activations, gradients, counts, in_basis, out_basis, previous):
    positions = jnp.arange(SEQ_LEN, dtype=jnp.int32)

    def accumulate(running, element):
        sequence, cotangent, length = element
        keep = (positions < length)[:, None]
        masked = jnp.where(keep, sequence, jnp.zeros_like(sequence))
        in_rotated = jnp.dot(masked, in_basis, preferred_element_type=jnp.float32).astype(jnp.bfloat16)
        out_rotated = jnp.dot(cotangent, out_basis, preferred_element_type=jnp.float32).astype(jnp.bfloat16)
        rotated = jnp.dot(out_rotated.T, in_rotated, preferred_element_type=jnp.float32)
        return running + rotated * rotated, None

    start = jnp.zeros((ORDER, ORDER), jnp.float32)
    power, unused = lax.scan(accumulate, start, (activations, gradients, counts))
    scaled = power / float(SEQS * SEQ_LEN)
    return 0.5 * previous + scaled.reshape(GRID_ROWS, TILE_R, ORDER)
```

```python
import functools

import jax
import jax.numpy as jnp
from jax import lax
from jax.experimental import pallas as pl
from jax.experimental.pallas import tpu as pltpu
from jax.sharding import PartitionSpec as P

MESH = pl.DeviceIdType.MESH
F32 = jnp.float32
BF16 = jnp.bfloat16

PARTS = ((0, 768), (768, 768), (1536, 512))
ORDERS = (("y", "x", "z"), ("x", "z", "y"), ("z", "x", "y"))
GATHERS = ((0, 768, "z", "x"), (768, 768, "x", "z"), (1536, 256, "z", "x"), (1792, 256, "x", "z"))


def kernel(
    count_ref, act_hbm, grad_hbm, inb_hbm, outb_hbm, out_hbm,
    act, grad, inb, outb, in_rot, out_rot, fin, *rest,
):
    bufs = [rest[8 * p: 8 * p + 8] for p in range(3)]
    (load_sem, core_s, core_r, a_s, a_r, b_s, b_r, s2_s, s2_r, s3_s, s3_r, g1_s, g1_r, g2_s, g2_r, out_sem) = rest[24:]
    dp, block = lax.axis_index("dp"), lax.axis_index("block")
    pos = {"y": dp // 2, "z": block // 4, "x": block % 4}
    core = dp % 2

    def shift(axis, by):
        return (pos[axis] + by) % 4

    def device(axis, by):
        here = dict(pos)
        here[axis] = shift(axis, by)
        return (here["y"] * 2 + core, here["z"] * 4 + here["x"])

    other_core = (pos["y"] * 2 + 1 - core, block)

    loads = []

    def load(src, dst):
        copy = pltpu.make_async_copy(src, dst, load_sem.at[len(loads)])
        copy.start()
        loads.append(copy)
        return copy

    load_act = load(act_hbm.at[0], act)
    load_inb = [load(inb_hbm.at[:, pl.ds(k * 512, 512)], inb.at[k]) for k in range(4)]
    load_grad = load(grad_hbm.at[0], grad)
    groups = (2, 1, 3, 0)
    load_outb = []
    for j, by in enumerate(groups):
        load_outb.append([
            load(
                outb_hbm.at[:, pl.ds(pl.multiple_of(r * 512 + shift("y", by) * 128, 128), 128)],
                outb.at[j, :, pl.ds(r * 128, 128)],
            )
            for r in range(4)
        ])

    barrier = pltpu.get_barrier_semaphore()
    pl.semaphore_signal(barrier, inc=1, device_id=other_core, device_id_type=MESH)
    for axis in "yxz":
        for by in (1, 2, 3):
            pl.semaphore_signal(barrier, inc=1, device_id=device(axis, by), device_id_type=MESH)

    started = []

    def send(src, dst, ssem, rsem, to):
        copy = pltpu.make_async_remote_copy(
            src_ref=src, dst_ref=dst, send_sem=ssem, recv_sem=rsem, device_id=to, device_id_type=MESH
        )
        copy.start()
        started.append(copy)
        return copy

    load_act.wait()
    keep = lax.broadcasted_iota(jnp.int32, (512, 1), 0) < count_ref[0]
    for k in range(4):
        load_inb[k].wait()
        for h in range(2):
            cols = slice(h * 256, (h + 1) * 256)
            got = jnp.dot(act[...], inb[k, :, cols], preferred_element_type=F32)
            in_rot[:, k * 512 + h * 256: k * 512 + (h + 1) * 256] = jnp.where(keep, got, 0.0).astype(BF16)
    load_grad.wait()

    def rotate_out(j):
        for copy in load_outb[j]:
            copy.wait()
        for h in range(2):
            got = jnp.dot(grad[...], outb[j, :, h * 256:(h + 1) * 256], preferred_element_type=F32).astype(BF16).T
            for i in range(2):
                r = h * 2 + i
                rows = pl.ds(pl.multiple_of(r * 512 + shift("y", groups[j]) * 128, 128), 128)
                out_rot[rows, :] = got[i * 128:(i + 1) * 128, :]

    def tile_rows(p, by, who):
        pieces = []
        base = who * 64
        if p == 0:
            for r in range(4):
                first = r * 512 + shift("y", by) * 128 + base
                pieces.append(out_rot[pl.ds(pl.multiple_of(first, 64), 64), :])
        elif p == 1:
            for g in range(4):
                for y in range(4):
                    first = shift("x", by) * 512 + y * 128 + base + g * 16
                    pieces.append(out_rot[pl.ds(pl.multiple_of(first, 16), 16), :])
        else:
            for r in range(4):
                for y in range(4):
                    first = r * 512 + y * 128 + base + shift("z", by) * 16
                    pieces.append(out_rot[pl.ds(pl.multiple_of(first, 16), 16), :])
        return jnp.concatenate(pieces, axis=0)

    core_copies = {}

    def tile(p, by):
        first, width = PARTS[p]
        own, xs, xr = bufs[p][:3]
        rows = jnp.concatenate([tile_rows(p, by, 1 - core), tile_rows(p, by, core)], axis=0)
        for c in range(0, width, 256):
            got = jnp.dot(rows, in_rot[:, first + c: first + c + 256], preferred_element_type=F32)
            got = got * got
            xs[by, :, c:c + 256] = got[:256].astype(BF16)
            own[by, :, c:c + 256] = got[256:]
        core_copies[p, by] = send(xs.at[by], xr.at[by], core_s.at[p, by], core_r.at[p, by], other_core)

    a_copies, b_copies = {}, {}
    low, high = slice(0, 128), slice(128, 256)

    def b_send(p, side, half):
        bs, br = bufs[p][5], bufs[p][6]
        rows = pl.ds(half * 128, 128)
        b_copies[p, side, half] = send(
            bs.at[side, rows], br.at[side, rows], b_s.at[p, side, half], b_r.at[p, side, half],
            device(ORDERS[p][0], (1, 3)[side]),
        )

    def finish(p, by):
        own, xs, xr, asend, arecv, bs, br, small = bufs[p]
        core_copies[p, by].wait_recv()
        if by == 2:
            asend[...] = (own[2] + xr[2].astype(F32)).astype(BF16)
            for half, to in ((0, 1), (1, 3)):
                a_copies[p, half] = send(
                    asend.at[pl.ds(half * 128, 128)], arecv.at[half], a_s.at[p, half], a_r.at[p, half],
                    device(ORDERS[p][0], to),
                )
        elif by == 0:
            own[0] = own[0] + xr[0].astype(F32)
        else:
            side = 0 if by == 1 else 1
            early = 1 - side
            rows = slice(early * 128, early * 128 + 128)
            bs[side, rows, :] = (own[by, rows, :] + xr[by, rows, :].astype(F32)).astype(BF16)
            b_send(p, side, early)

    def late(p, side):
        own, xs, xr, asend, arecv, bs, br, small = bufs[p]
        by = (1, 3)[side]
        rows = slice(side * 128, side * 128 + 128)
        a_copies[p, side].wait_recv()
        total = own[by, rows, :] + xr[by, rows, :].astype(F32) + arecv[side].astype(F32)
        bs[side, rows, :] = total.astype(BF16)
        b_send(p, side, side)

    s2_copies, s3_copies = {}, {}

    def stage1(p):
        own, xs, xr, asend, arecv, bs, br, small = bufs[p]
        s2send, s2recv, s2sum, s3recv = small
        for key in ((0, 0), (0, 1), (1, 0), (1, 1)):
            b_copies[p, key[0], key[1]].wait_recv()
        own[0] = own[0] + br[0].astype(F32) + br[1].astype(F32)
        axis = ORDERS[p][1]
        for by in (2, 1, 3):
            rows = pl.ds(pl.multiple_of(shift(axis, by) * 64, 64), 64)
            s2send[by - 1] = own[0, rows, :].astype(BF16)
            s2_copies[p, by] = send(
                s2send.at[by - 1], s2recv.at[by - 1], s2_s.at[p, by - 1], s2_r.at[p, by - 1], device(axis, by)
            )

    def stage2(p):
        own, xs, xr, asend, arecv, bs, br, small = bufs[p]
        s2send, s2recv, s2sum, s3recv = small
        for by in (1, 2, 3):
            s2_copies[p, by].wait_recv()
        rows = pl.ds(pl.multiple_of(pos[ORDERS[p][1]] * 64, 64), 64)
        s2sum[...] = own[0, rows, :] + s2recv[0].astype(F32) + s2recv[1].astype(F32) + s2recv[2].astype(F32)
        axis = ORDERS[p][2]
        for by in (2, 1, 3):
            rows = pl.ds(pl.multiple_of(shift(axis, by) * 16, 16), 16)
            s3_copies[p, by] = send(
                s2sum.at[rows], s3recv.at[by - 1], s3_s.at[p, by - 1], s3_r.at[p, by - 1], device(axis, by)
            )

    def stage3(p):
        first, width = PARTS[p]
        s2send, s2recv, s2sum, s3recv = bufs[p][7]
        for by in (1, 2, 3):
            s3_copies[p, by].wait_recv()
        rows = pl.ds(pl.multiple_of(pos[ORDERS[p][2]] * 16, 16), 16)
        fin[pos["x"], pos["z"], :, first:first + width] = s2sum[rows, :] + s3recv[0] + s3recv[1] + s3recv[2]

    g1_copies, g2_copies = {}, {}

    def gather1(g):
        first, width, axis, unused = GATHERS[g]
        ref = fin.at[pos["x"], pos["z"], :, pl.ds(first, width)]
        for by in (2, 1, 3):
            g1_copies[g, by] = send(ref, ref, g1_s.at[g, by - 1], g1_r.at[g, by - 1], device(axis, by))

    def gather2(g):
        first, width, unused, axis = GATHERS[g]
        for by in (1, 2, 3):
            g1_copies[g, by].wait_recv()
        if axis == "x":
            ref = fin.at[pos["x"], :, :, pl.ds(first, width)]
        else:
            ref = fin.at[:, pos["z"], :, pl.ds(first, width)]
        for by in (2, 1, 3):
            g2_copies[g, by] = send(ref, ref, g2_s.at[g, by - 1], g2_r.at[g, by - 1], device(axis, by))

    outs = []

    def write(g):
        first, width = GATHERS[g][:2]
        for by in (1, 2, 3):
            g2_copies[g, by].wait_recv()
        copy = pltpu.make_async_copy(
            fin.at[:, :, :, pl.ds(first, width)], out_hbm.at[:, :, :, pl.ds(first, width)], out_sem.at[g]
        )
        copy.start()
        outs.append(copy)

    rotate_out(0)
    pl.semaphore_wait(barrier, 10)
    tile(0, 2)
    rotate_out(1)
    finish(0, 2)
    rotate_out(2)
    rotate_out(3)
    order = [(1, 2), (2, 2), (0, 1), (0, 3), (1, 1), (1, 3), (2, 1), (2, 3), (0, 0), (1, 0), (2, 0)]
    for n, key in enumerate(order):
        tile(*key)
        if n:
            finish(*order[n - 1])
    finish(*order[-1])
    for p in range(3):
        late(p, 0)
        late(p, 1)
    for p in range(3):
        stage1(p)
    for p in range(3):
        stage2(p)
    stage3(0)
    gather1(0)
    stage3(1)
    gather1(1)
    stage3(2)
    gather1(2)
    gather1(3)
    for g in range(4):
        gather2(g)
    for g in range(4):
        write(g)
    for copy in started:
        copy.wait_send()
    for copy in outs:
        copy.wait()


def scratch():
    shapes = [
        pltpu.VMEM((512, 2048), BF16),
        pltpu.VMEM((512, 2048), BF16),
        pltpu.VMEM((4, 2048, 512), BF16),
        pltpu.VMEM((4, 2048, 512), BF16),
        pltpu.VMEM((512, 2048), BF16),
        pltpu.VMEM((2048, 512), BF16),
        pltpu.VMEM((4, 4, 16, 2048), F32),
    ]
    for first, width in PARTS:
        shapes += [
            pltpu.VMEM((4, 256, width), F32),
            pltpu.VMEM((4, 256, width), BF16),
            pltpu.VMEM((4, 256, width), BF16),
            pltpu.VMEM((256, width), BF16),
            pltpu.VMEM((2, 128, width), BF16),
            pltpu.VMEM((2, 256, width), BF16),
            pltpu.VMEM((2, 256, width), BF16),
            (
                pltpu.VMEM((3, 64, width), BF16),
                pltpu.VMEM((3, 64, width), BF16),
                pltpu.VMEM((64, width), F32),
                pltpu.VMEM((3, 16, width), F32),
            ),
        ]
    dma = pltpu.SemaphoreType.DMA
    shapes += [dma((22,))]
    for shape in ((3, 4), (3, 2), (3, 2, 2), (3, 3), (3, 3), (4, 3), (4, 3)):
        shapes += [dma(shape), dma(shape)]
    shapes += [dma((4,))]
    return shapes


def body(activations, gradients, counts, in_basis, out_basis, previous):
    hbm = pl.BlockSpec(memory_space=pl.ANY)
    power = pl.pallas_call(
        kernel,
        out_shape=jax.ShapeDtypeStruct((4, 4, 16, 2048), F32),
        in_specs=[pl.BlockSpec(memory_space=pltpu.SMEM), hbm, hbm, hbm, hbm],
        out_specs=hbm,
        scratch_shapes=scratch(),
        compiler_params=pltpu.CompilerParams(
            collective_id=0, has_side_effects=True, vmem_limit_bytes=62 * 2 ** 20
        ),
    )(counts, activations, gradients, in_basis, out_basis)
    return 0.5 * previous + power.reshape(4, 64, 2048) / 65536.0


def solution(mesh):
    return jax.shard_map(
        body,
        mesh=mesh,
        in_specs=(
            P(("dp", "block"), None, None),
            P(("dp", "block"), None, None),
            P(("dp", "block")),
            P(),
            P(),
            P(None, "dp", None),
        ),
        out_specs=P(None, "dp", None),
        check_vma=False,
    )
```
